128 devices in a mesh: phase: 4 (over x), grp: 4 (over z_hi, core), tp: 8 (over z_lo, y).
Axes of the slice: x: 4, y: 4, z: 4 (z_hi: 2, z_lo: 2; z = z_hi * 2 + z_lo), core: 2. Of those that a mesh axis runs over, the one named last changes fastest.
Arguments:
- prompt_embed: bfloat16 [512, 8192], P('grp', 'tp'), may hold values from -6 to 6
- prompt_lengths: int32 [4, 4], replicated, may hold values from 1 to 64, 128 in all within a row
- decode_group: int32 [4, 4, 1], replicated, may hold values from 0 to 3; in each aligned block of 4 rows (0 to 3, 4 to 7, ..., all dimensions but the last counted through in order) at most 2 rows name the same one
- step_embed: bfloat16 [4, 16, 8192], P(None, 'grp', 'tp'), may hold values from -6 to 6
- norm_gain: float32 [4, 8192], P('phase'), may hold values from 0.5 to 1.5
- w_query: bfloat16 [4, 8192, 4096], P('phase', None, 'tp'), may hold values from -0.0625 to 0.0625
- w_key: bfloat16 [4, 8192, 1024], P('phase', None, 'tp'), may hold values from -0.0625 to 0.0625
- w_value: bfloat16 [4, 8192, 1024], P('phase', None, 'tp'), may hold values from -0.0625 to 0.0625
- w_out: bfloat16 [4, 4096, 8192], P('phase', 'tp'), may hold values from -0.09375 to 0.09375
Outputs:
- prefill_out: bfloat16 [4, 512, 8192], P('phase', 'grp', 'tp')
- decode_out: bfloat16 [4, 4, 32, 8192], P('phase', None, 'grp', 'tp')
The draws below stay inside these ranges and needn't reach their ends.
Inputs may be any that keep to these rules, and one draw needn't show every extreme that they name: `prompt_lengths`: the 4 prompts of one prefill device fill its 128 rows; the longest has 64 tokens. `decode_group`: at most 2 prompts of one prefill device go to the same decode device, and some device sends exactly 2 to one.
All inputs are finite; a program needn't handle non-finite values.
Results may differ from the reference program's by a relative error of at most 0.023.
Values may be sent and summed in bfloat16 or wider, within the bound.
A program may use at most 128 MiB of HBM per device.

```python
import math
import jax
import jax.numpy as jnp
import numpy as np
from jax import lax

D = 8192
HQ = 32
KVH = 8
HD = 128
PTOK = 128
DOCS = 4
CAP = 2
STEPS = 4
MAXLEN = 64
TOKENS = 512
REQUESTS = 16
N_PHASE = 4
N_GRP = 4


def steps_of(own_key, shape, shards, smallest, high):
    def one(axis_at, blocks):
        heights = jax.random.uniform(jax.random.fold_in(jax.random.fold_in(own_key, 6), axis_at), (blocks,), jnp.float32, smallest / len(shards), high / len(shards))
        return jnp.repeat(jnp.exp(heights), shape[axis_at] // blocks).reshape((-1,) + (1,) * (len(shape) - axis_at - 1))

    factor_of = one(*shards[0])
    for cut in shards[1:]:
        factor_of = factor_of * one(*cut)
    return factor_of


def split_up(amount, total, most, skew):
    weights = [(1 << 20) // math.isqrt(grade ** skew) + 1 for grade in range(2, amount + 1)]
    surplus, given = total - most - (amount - 1), [1] * (amount - 1)
    while surplus > 0:
        movable = [i for i in range(amount - 1) if given[i] < most]
        mass, remaining = sum([weights[i] for i in movable]), surplus
        for i in movable:
            more = min(most - given[i], max(1, remaining * weights[i] // mass), surplus)
            given[i] = given[i] + more
            surplus = surplus - more
    return np.array([most] + given)


def ragged_sizes(key, count, total, reach, slope):
    if count == 2:
        one = jax.random.randint(key, (), max(1, total - reach), min(reach, total - 1) + 1)
        return jnp.stack([one, total - one])
    lengths = jnp.asarray(split_up(count, total, reach, slope), jnp.int32)
    couples = (count - 1) // 2
    giver, taker = lengths[1:1 + 2 * couples:2], lengths[2:2 + 2 * couples:2]
    margin = jnp.minimum(giver - 1, reach - taker)
    shifted = jax.random.randint(jax.random.fold_in(key, 1), (couples,), 0, 1 << 20) % (margin + 1)
    lengths = lengths.at[1:1 + 2 * couples:2].set(giver - shifted).at[2:2 + 2 * couples:2].set(taker + shifted)
    return lengths[jax.random.permutation(jax.random.fold_in(key, 2), count)]


def shared_out(rng, own, number, rows, count, top, reach, skew):
    ranking = jax.random.permutation(rng, count)
    heavy_load, common = load_shares(count, rows * top, reach, skew, True), load_shares(count, rows * top, reach, skew, False)
    places = jnp.arange(count)

    def named(tallies, rotation):
        used = int((tallies > 0).sum())
        fixed = max(1, used // 4)
        moved = fixed + (places - fixed + rotation * (used - fixed)) % max(1, count - fixed)
        return jnp.zeros((count,), jnp.int32).at[ranking[jnp.where(places < fixed, places, moved)]].set(jnp.asarray(tallies, jnp.int32))

    tallies = jnp.where(number % 4 == 0, named(heavy_load, number // 4), named(common, number - number // 4 - 1))
    mixed = jax.random.permutation(jax.random.fold_in(own, 3), count)
    giver, sink = mixed[0:count // 2 * 2:2], mixed[1:count // 2 * 2:2]
    slack = jnp.minimum(tallies[giver] - 1, reach - tallies[sink]) // 2
    slack = jnp.where((giver == ranking[0]) | (sink == ranking[0]) | (tallies[sink] == 0), 0, jnp.maximum(slack, 0))
    moved = jax.random.randint(jax.random.fold_in(own, 4), (count // 2,), 0, 1 << 20) % (slack + 1)
    tallies = tallies.at[giver].add(-moved).at[sink].add(moved)
    members = jnp.searchsorted(jnp.cumsum(tallies), jnp.arange(rows * top), side="right").astype(jnp.int32)
    listing = members.reshape(top, rows).T
    listing = listing[jax.random.permutation(jax.random.fold_in(own, 1), rows)]
    rotation = jax.random.randint(jax.random.fold_in(own, 2), (rows, 1), 0, top)
    return jnp.take_along_axis(listing, (jnp.arange(top)[None, :] + rotation) % top, axis=1)


def load_shares(amount, total, bound, skew, full):
    weights = [(1 << 20) // math.isqrt(grade ** skew) + 1 for grade in range(1, amount + 1)]
    largest = bound if full else min(bound, max(-(-total // amount), total * weights[0] // sum(weights)))
    least = 1 if total - largest >= amount - 1 else 0
    given, surplus = [largest] + [least] * (amount - 1), total - largest - least * (amount - 1)
    while surplus > 0:
        candidates = [i for i in range(1, amount) if given[i] < largest] or [i for i in range(1, amount) if given[i] < bound]
        whole, left = sum([weights[i] for i in candidates]), surplus
        for i in candidates:
            more = min(bound - given[i], max(1, left * weights[i] // whole), surplus)
            given[i] = given[i] + more
            surplus = surplus - more
    return np.array(given)


def centred(own_key, extent, width, limit, shards=(), kind=jnp.bfloat16):
    gain = steps_of(own_key, extent, shards, -0.22, 0.18) if shards else 1.0
    array = jax.random.normal(own_key, extent, jnp.float32) * width * gain
    return jnp.minimum(jnp.maximum(array, -limit), limit).astype(kind)


def setup_inputs(seed: int = 0) -> dict:
    splits = jax.random.split(jax.random.key(seed), 10)
    prompt_embed = centred(splits[0], (TOKENS, D), 1.0, 6.0, ((0, 4), (1, 8)))
    prompt_lengths = jax.vmap(lambda own: ragged_sizes(own, DOCS, PTOK, MAXLEN, 2))(jax.random.split(splits[1], N_GRP)).reshape((N_GRP, DOCS)).astype(jnp.int32)
    decode_group_keys = jax.random.split(jax.random.fold_in(splits[2], 1), N_GRP * DOCS // DOCS)
    decode_group_turns = jax.random.permutation(jax.random.fold_in(splits[2], 3), N_GRP * DOCS // DOCS)
    decode_group = jax.vmap(lambda own, number: shared_out(jax.random.fold_in(splits[2], 2), own, number, DOCS, N_GRP, 1, CAP, 2))(decode_group_keys, decode_group_turns).reshape((N_GRP, DOCS, 1))
    step_embed = centred(splits[3], (STEPS, REQUESTS, D), 1.0, 6.0, ((1, 4), (2, 8)))
    norm_gain = jnp.clip(1.0 + 0.1 * jax.random.normal(splits[4], (N_PHASE, D), jnp.float32), 0.5, 1.5)
    w_query = centred(splits[5], (N_PHASE, D, HQ * HD), D ** -0.5, 0.0625, ((0, 4), (2, 8)))
    w_key = centred(splits[6], (N_PHASE, D, KVH * HD), D ** -0.5, 0.0625, ((0, 4), (2, 8)))
    w_value = centred(splits[7], (N_PHASE, D, KVH * HD), D ** -0.5, 0.0625, ((0, 4), (2, 8)))
    w_out = centred(splits[8], (N_PHASE, HQ * HD, D), (HQ * HD) ** -0.5, 0.09375, ((0, 4), (1, 8)))
    return {"prompt_embed": prompt_embed, "prompt_lengths": prompt_lengths, "decode_group": decode_group, "step_embed": step_embed, "norm_gain": norm_gain, "w_query": w_query, "w_key": w_key, "w_value": w_value, "w_out": w_out}


EPS = 1e-06
THETA = 1000000.0

def rotate(values, places):
    half_dim = values.shape[-1] // 2
    frequency = THETA ** (-2.0 * jnp.arange(half_dim, dtype=jnp.float32) / values.shape[-1])
    angles = places[..., None, None] * frequency
    cosine = jnp.cos(angles)
    sine_part = jnp.sin(angles)
    first_half = values[..., :half_dim]
    second_half = values[..., half_dim:]
    return jnp.concatenate([first_half * cosine - second_half * sine_part, second_half * cosine + first_half * sine_part], axis=-1)

def normed(hidden, gain_row):
    values = hidden.astype(jnp.float32)
    factor = lax.rsqrt(lax.optimization_barrier(jnp.mean(values * values, axis=-1, keepdims=True)) + EPS)
    return (values * factor * gain_row).astype(jnp.bfloat16)

def softmax_rows(scores, allowed):
    masked = jnp.where(allowed, scores, -1e+30)
    return jax.nn.softmax(masked, axis=-1).astype(jnp.bfloat16)

def reference(prompt_embed, prompt_lengths, decode_group, step_embed, norm_gain, w_query, w_key, w_value, w_out):
    per_group = HQ // KVH
    score_scale = 1.0 / math.sqrt(HD)
    doc_ends = jnp.cumsum(prompt_lengths, axis=1).astype(jnp.int32)
    starts = doc_ends - prompt_lengths
    places = jnp.arange(PTOK, dtype=jnp.int32)
    segment = lax.optimization_barrier(jnp.sum((places[None, :, None] >= doc_ends[:, None, :]).astype(jnp.int32), axis=-1))
    local_pos = places[None, :] - jnp.take_along_axis(starts, segment, axis=1)
    positions = local_pos.reshape(-1).astype(jnp.float32)
    allowed = (segment[:, :, None] == segment[:, None, :]) & (places[None, :, None] >= places[None, None, :])
    hidden = prompt_embed
    layer_keys = []
    layer_values = []
    prefill_out = []
    for layer_idx in range(N_PHASE):
        normal_rows = normed(hidden, norm_gain[layer_idx])
        queries = jnp.dot(normal_rows, w_query[layer_idx], preferred_element_type=jnp.float32).reshape(-1, HQ, HD)
        new_keys = jnp.dot(normal_rows, w_key[layer_idx], preferred_element_type=jnp.float32).reshape(-1, KVH, HD)
        new_values = jnp.dot(normal_rows, w_value[layer_idx], preferred_element_type=jnp.float32).astype(jnp.bfloat16).reshape(N_GRP, PTOK, KVH, HD)
        queries = rotate(queries, positions).astype(jnp.bfloat16).reshape(N_GRP, PTOK, KVH, per_group, HD)
        new_keys = rotate(new_keys, positions).astype(jnp.bfloat16).reshape(N_GRP, PTOK, KVH, HD)
        scores = jnp.einsum('bqkgd,bskd->bkgqs', queries.astype(jnp.float32), new_keys.astype(jnp.float32)) * score_scale
        probability = softmax_rows(scores, allowed[:, None, None])
        head_out = jnp.einsum('bkgqs,bskd->bqkgd', probability.astype(jnp.float32), new_values.astype(jnp.float32)).astype(jnp.bfloat16).reshape(-1, HQ * HD)
        hidden = (hidden.astype(jnp.float32) + jnp.dot(head_out, w_out[layer_idx], preferred_element_type=jnp.float32)).astype(jnp.bfloat16)
        layer_keys.append(new_keys.reshape(N_GRP * PTOK, KVH, HD))
        layer_values.append(new_values.reshape(N_GRP * PTOK, KVH, HD))
        prefill_out.append(hidden)
    assign = decode_group[:, :, 0]
    doc_ids = jnp.arange(DOCS, dtype=jnp.int32)
    earlier = doc_ids[:, None] > doc_ids[None, :]
    slot_rank = lax.optimization_barrier(jnp.sum(((assign[:, :, None] == assign[:, None, :]) & earlier[None]).astype(jnp.int32), axis=-1))
    sources = jnp.arange(N_GRP, dtype=jnp.int32)[:, None]
    slot_ids = (assign * (N_GRP * CAP) + sources * CAP + slot_rank).reshape(-1).astype(jnp.int32)
    request_len = prompt_lengths.reshape(-1)
    offset = jnp.arange(MAXLEN, dtype=jnp.int32)
    row_ids = (sources[:, :, None] * PTOK + jnp.minimum(starts[:, :, None] + offset, PTOK - 1)).reshape(-1).astype(jnp.int32)
    inside = offset[None, :] < request_len[:, None]
    requests = N_GRP * DOCS
    cache_keys = []
    cache_values = []
    for layer_idx in range(N_PHASE):
        picked_keys = layer_keys[layer_idx][row_ids].reshape(requests, MAXLEN, KVH, HD)
        picked_values = layer_values[layer_idx][row_ids].reshape(requests, MAXLEN, KVH, HD)
        cache_keys.append(jnp.where(inside[:, :, None, None], picked_keys, jnp.zeros_like(picked_keys)))
        cache_values.append(jnp.where(inside[:, :, None, None], picked_values, jnp.zeros_like(picked_values)))
    fresh_keys = [jnp.zeros((requests, STEPS, KVH, HD), jnp.bfloat16) for layer_idx in range(N_PHASE)]
    fresh_values = [jnp.zeros((requests, STEPS, KVH, HD), jnp.bfloat16) for layer_idx in range(N_PHASE)]
    decode_out = jnp.zeros((N_PHASE, STEPS, N_GRP * N_GRP * CAP, D), jnp.bfloat16)
    step_ids = jnp.arange(STEPS, dtype=jnp.int32)
    for step_idx in range(STEPS):
        hidden = step_embed[step_idx]
        places_now = (request_len + step_idx).astype(jnp.float32)
        allowed_now = jnp.concatenate([inside, jnp.broadcast_to(step_ids[None, :] <= step_idx, (requests, STEPS))], axis=1)
        for layer_idx in range(N_PHASE):
            normal_rows = normed(hidden, norm_gain[layer_idx])
            queries = jnp.dot(normal_rows, w_query[layer_idx], preferred_element_type=jnp.float32).reshape(requests, HQ, HD)
            queries = rotate(queries, places_now).astype(jnp.bfloat16).reshape(requests, KVH, per_group, HD)
            new_key = jnp.dot(normal_rows, w_key[layer_idx], preferred_element_type=jnp.float32).reshape(requests, KVH, HD)
            new_key = rotate(new_key, places_now).astype(jnp.bfloat16)
            new_value = jnp.dot(normal_rows, w_value[layer_idx], preferred_element_type=jnp.float32).astype(jnp.bfloat16).reshape(requests, KVH, HD)
            fresh_keys[layer_idx] = fresh_keys[layer_idx].at[:, step_idx].set(new_key)
            fresh_values[layer_idx] = fresh_values[layer_idx].at[:, step_idx].set(new_value)
            all_keys = jnp.concatenate([cache_keys[layer_idx], fresh_keys[layer_idx]], axis=1)
            all_values = jnp.concatenate([cache_values[layer_idx], fresh_values[layer_idx]], axis=1)
            scores = jnp.einsum('rkgd,rskd->rkgs', queries.astype(jnp.float32), all_keys.astype(jnp.float32)) * score_scale
            probability = softmax_rows(scores, allowed_now[:, None, None])
            head_out = jnp.einsum('rkgs,rskd->rkgd', probability.astype(jnp.float32), all_values.astype(jnp.float32)).astype(jnp.bfloat16).reshape(requests, HQ * HD)
            hidden = (hidden.astype(jnp.float32) + jnp.dot(head_out, w_out[layer_idx], preferred_element_type=jnp.float32)).astype(jnp.bfloat16)
            decode_out = decode_out.at[layer_idx, step_idx, slot_ids].set(hidden)
    return (jnp.stack(prefill_out), decode_out)
```

```python
import functools
import math

import jax
import jax.numpy as jnp
from jax import lax
from jax.experimental import pallas as pl
from jax.experimental.pallas import tpu as pltpu
from jax.sharding import PartitionSpec as P

D = 8192
HQ = 4
HD = 128
STEPS = 4
DOCS = 4
CAP = 2
N_TP = 8
N_GRP = 4
N_PHASE = 4
PTOK = 128
ROWS = PTOK + STEPS * DOCS
CH = D // N_TP
NQKV = (HQ + 2) * HD
KEYS = 256
EPS = 1e-06
THETA = 1000000.0
MESH = pl.DeviceIdType.MESH

SIZES = (32, 32, 32, 32, 16)
STARTS = tuple(sum(SIZES[:i]) for i in range(len(SIZES)))
NB = len(SIZES)
RMAX = max(SIZES)


def kernel(
    lens_ref, dest_ref, x_ref, steps_ref, gain_ref, wq_hbm, wk_hbm, wv_hbm, wo_hbm,
    pre_out, dec_out,
    w, wo, xg, rs, st, xo, own, acc, ssq, hb, kb, vb, cosb, sinb, bias, dsend, drecv,
    wsem, first_send, ag_send, ag_recv, rs_send, rs_recv, dec_send, dec_recv,
):
    phase = lax.axis_index("phase")
    grp = lax.axis_index("grp")
    me = lax.axis_index("tp")
    my_y, my_z = me % 4, me // 4

    def peer(k):
        return ((my_z + k // 4) % 2) * 4 + (my_y + k % 4) % 4

    def weight_copies(c):
        rows = pl.ds(c * CH, CH)
        return (
            pltpu.make_async_copy(wq_hbm.at[rows], w.at[rows, pl.ds(0, HQ * HD)], wsem.at[0, c]),
            pltpu.make_async_copy(wk_hbm.at[rows], w.at[rows, pl.ds(HQ * HD, HD)], wsem.at[1, c]),
            pltpu.make_async_copy(wv_hbm.at[rows], w.at[rows, pl.ds(HQ * HD + HD, HD)], wsem.at[2, c]),
        )

    def out_weight_copy(c):
        cols = pl.ds(pl.multiple_of(c * CH, CH), CH)
        return pltpu.make_async_copy(wo_hbm.at[:, cols], wo.at[:, cols], wsem.at[3, c])

    @pl.loop(0, N_TP)
    def _(k):
        for copy in weight_copies(peer(k)):
            copy.start()

    @pl.loop(0, N_TP)
    def _(k):
        out_weight_copy(peer(N_TP - 1 - k)).start()

    barrier = pltpu.get_barrier_semaphore()

    def greet(device):
        pl.semaphore_signal(barrier, inc=1, device_id=device, device_id_type=MESH)

    for k in range(1, N_TP):
        greet((phase, grp, peer(k)))
    for k in range(1, N_GRP):
        greet((phase, (grp + k) % N_GRP, me))

    @pl.when(phase > 0)
    def _():
        for k in range(N_TP):
            greet((phase - 1, grp, peer(k)))

    @pl.when(phase < N_PHASE - 1)
    def _():
        for k in range(N_TP):
            greet((phase + 1, grp, peer(k)))

    lens = [lens_ref[grp, d] for d in range(DOCS)]
    starts = [jnp.int32(0)]
    for d in range(DOCS):
        starts.append(starts[-1] + lens[d])

    def pick(values, index):
        out = jnp.full(index.shape, values[-1], jnp.int32)
        for d in range(DOCS - 1):
            out = jnp.where(index == d, values[d], out)
        return out

    def segment_and_place(row):
        of_prompt = sum((row >= starts[d]).astype(jnp.int32) for d in range(1, DOCS))
        of_step = (row - PTOK) & (DOCS - 1)
        step = (row - PTOK) >> 2
        segment = jnp.where(row < PTOK, of_prompt, of_step)
        place = jnp.where(row < PTOK, row - pick(starts[:DOCS], of_prompt), pick(lens, of_step) + step)
        return jnp.where(row < ROWS, segment, -1), place

    seg_q, place_q = segment_and_place(lax.broadcasted_iota(jnp.int32, (ROWS, HD), 0))
    lane = lax.broadcasted_iota(jnp.int32, (ROWS, HD), 1)
    half = (lane & (HD // 2 - 1)).astype(jnp.float32)
    angle = place_q.astype(jnp.float32) * jnp.exp(half * (-2.0 / HD * math.log(THETA)))
    cosb[...] = jnp.cos(angle)
    sine = jnp.sin(angle)
    sinb[...] = jnp.where(lane < HD // 2, -sine, sine)
    for part in range(KEYS // HD):
        seg_k, place_k = segment_and_place(lax.broadcasted_iota(jnp.int32, (ROWS, HD), 1) + part * HD)
        bias[:, part * HD : (part + 1) * HD] = jnp.where((seg_q == seg_k) & (place_k <= place_q), 0.0, -1e30)
    kb[...] = jnp.zeros_like(kb)
    vb[...] = jnp.zeros_like(vb)

    @pl.when(phase == 0)
    def _():
        xg[me, 0:PTOK] = x_ref[...]
        xg[me, PTOK:ROWS] = steps_ref[...]

    middle = ((phase > 0) & (phase < N_PHASE - 1)).astype(jnp.int32)
    pl.semaphore_wait(barrier, N_TP - 1 + N_GRP - 1 + N_TP + N_TP * middle)

    def first_copy(b, k):
        rows = pl.ds(STARTS[b], SIZES[b])
        return pltpu.make_async_remote_copy(
            src_ref=xg.at[me, rows], dst_ref=xg.at[me, rows],
            send_sem=first_send.at[b, k], recv_sem=ag_recv.at[b, me],
            device_id=(0, grp, peer(N_TP - k)), device_id_type=MESH)

    def next_copy(b, k):
        rows = pl.ds(STARTS[b], SIZES[b])
        return pltpu.make_async_remote_copy(
            src_ref=xo.at[rows], dst_ref=xg.at[me, rows],
            send_sem=ag_send.at[b, k], recv_sem=ag_recv.at[b, me],
            device_id=(phase + 1, grp, peer(k)), device_id_type=MESH)

    def part_copy(b, k):
        rows = pl.ds(STARTS[b], SIZES[b])
        return pltpu.make_async_remote_copy(
            src_ref=st.at[k, rows], dst_ref=rs.at[me, rows],
            send_sem=rs_send.at[b, k], recv_sem=rs_recv.at[b, me],
            device_id=(phase, grp, peer(k)), device_id_type=MESH)

    def arrival(buffer, sems, b, c):
        rows = pl.ds(STARTS[b], SIZES[b])
        return pltpu.make_async_remote_copy(
            src_ref=buffer.at[c, rows], dst_ref=buffer.at[c, rows],
            send_sem=rs_send.at[b, 0], recv_sem=sems.at[b, c],
            device_id=(phase, grp, peer(1)), device_id_type=MESH)

    def first_sends(b):
        if b < NB:
            @pl.when(phase == 0)
            def _():
                for k in range(1, N_TP):
                    first_copy(b, k).start()

    def project_in(b):
        first, size = STARTS[b], SIZES[b]
        acc[0:size] = jnp.zeros((size, NQKV), jnp.float32)
        ssq[0:size] = jnp.zeros((size, HD), jnp.float32)

        @pl.loop(0, N_TP)
        def _(k):
            c = peer(k)

            @pl.when((phase > 0) | (k > 0))
            def _():
                arrival(xg, ag_recv, b, c).wait_recv()

            if b == 0:
                for copy in weight_copies(c):
                    copy.wait()
            values = xg[c, first : first + size, :].astype(jnp.float32)
            squares = values * values
            ssq[0:size] += sum(squares[:, i * HD : (i + 1) * HD] for i in range(CH // HD))
            scaled = (values * gain_ref[:, pl.ds(pl.multiple_of(c * CH, CH), CH)]).astype(jnp.bfloat16)
            acc[0:size] += jnp.dot(scaled, w[pl.ds(c * CH, CH), :], preferred_element_type=jnp.float32)

    def attend(b):
        first, size = STARTS[b], SIZES[b]
        rows = slice(first, first + size)
        factor = lax.rsqrt(jnp.sum(ssq[0:size], axis=-1, keepdims=True) * (1.0 / D) + EPS)
        cosine, sine = cosb[rows], sinb[rows]

        def rotated(values):
            return (values * cosine + pltpu.roll(values, HD // 2, 1) * sine).astype(jnp.bfloat16)

        projected = acc[0:size] * factor
        heads = [rotated(projected[:, h * HD : (h + 1) * HD]) for h in range(HQ + 1)]
        kb[rows] = heads[HQ]
        vb[rows] = projected[:, (HQ + 1) * HD :].astype(jnp.bfloat16)
        n_keys = HD if first + size <= HD else KEYS
        queries = jnp.concatenate(heads[:HQ], axis=0)
        scores = lax.dot_general(
            queries, kb[0:n_keys], (((1,), (1,)), ((), ())), preferred_element_type=jnp.float32)
        mask = bias[rows, 0:n_keys]
        scores = scores * (1.0 / math.sqrt(HD)) + jnp.concatenate([mask] * HQ, axis=0)
        raised = jnp.exp(scores - jnp.max(scores, axis=-1, keepdims=True))
        probability = (raised / jnp.sum(raised, axis=-1, keepdims=True)).astype(jnp.bfloat16)
        mixed = jnp.dot(probability, vb[0:n_keys], preferred_element_type=jnp.float32).astype(jnp.bfloat16)
        for h in range(HQ):
            hb[0:size, h * HD : (h + 1) * HD] = mixed[h * size : (h + 1) * size]

    def project_out(b):
        first, size = STARTS[b], SIZES[b]

        def product(k):
            c = peer(k)
            if b == 0:
                out_weight_copy(c).wait()
            cols = pl.ds(pl.multiple_of(c * CH, CH), CH)
            return jnp.dot(hb[0:size], wo[:, cols], preferred_element_type=jnp.float32)

        @pl.loop(0, N_TP - 1)
        def _(j):
            k = N_TP - 1 - j
            st[k, first : first + size] = product(k).astype(jnp.bfloat16)
            part_copy(b, k).start()

        own[0:size] = product(0)

    def finish(b):
        first, size = STARTS[b], SIZES[b]
        rows = slice(first, first + size)
        own[0:size] += xg[me, rows].astype(jnp.float32)

        @pl.loop(1, N_TP)
        def _(k):
            c = peer(k)
            arrival(rs, rs_recv, b, c).wait_recv()
            own[0:size] += rs[c, rows].astype(jnp.float32)

        result = own[0:size].astype(jnp.bfloat16)
        xo[rows] = result

        @pl.when(phase < N_PHASE - 1)
        def _():
            for k in range(N_TP - 1, -1, -1):
                next_copy(b, k).start()

        inside = min(first + size, PTOK) - first
        if inside > 0:
            pre_out[first : first + inside] = result[0:inside]

    first_sends(0)
    for b in range(NB):
        first_sends(b + 1)
        project_in(b)
        attend(b)
        project_out(b)
        finish(b)

    row = lax.broadcasted_iota(jnp.int32, (N_GRP * STEPS * CAP, STEPS * DOCS), 0)
    col = lax.broadcasted_iota(jnp.int32, (N_GRP * STEPS * CAP, STEPS * DOCS), 1)
    dests = [dest_ref[grp, d] for d in range(DOCS)]
    ranks = [
        sum([(dests[e] == dests[d]).astype(jnp.int32) for e in range(d)], jnp.int32(0)) for d in range(DOCS)
    ]
    doc = col & (DOCS - 1)
    chosen = (
        (pick(dests, doc) == (row >> 3)) & (pick(ranks, doc) == (row & 1)) & ((col >> 2) == ((row >> 1) & 3))
    )
    chosen = jnp.where(chosen, 1.0, 0.0).astype(jnp.bfloat16)
    picked = jnp.dot(chosen, xo[PTOK:ROWS], preferred_element_type=jnp.float32)
    dsend[...] = picked.reshape(N_GRP, STEPS * CAP, CH)
    drecv[grp] = dsend[grp]

    def decode_copy(k):
        to = (grp + k) % N_GRP
        return pltpu.make_async_remote_copy(
            src_ref=dsend.at[to], dst_ref=drecv.at[grp],
            send_sem=dec_send.at[k], recv_sem=dec_recv.at[k],
            device_id=(phase, to, me), device_id_type=MESH)

    for k in range(1, N_GRP):
        decode_copy(k).start()

    @pl.when(phase == 0)
    def _():
        for b in range(NB):
            for k in range(1, N_TP):
                first_copy(b, k).wait_send()

    @pl.when(phase < N_PHASE - 1)
    def _():
        for b in range(NB):
            for k in range(N_TP):
                next_copy(b, k).wait_send()

    for b in range(NB):
        for k in range(1, N_TP):
            part_copy(b, k).wait_send()

    for k in range(1, N_GRP):
        came = (grp + N_GRP - k) % N_GRP
        pltpu.make_async_remote_copy(
            src_ref=dsend.at[came], dst_ref=drecv.at[came],
            send_sem=dec_send.at[k], recv_sem=dec_recv.at[k],
            device_id=(phase, came, me), device_id_type=MESH).wait_recv()
        decode_copy(k).wait_send()
    n = N_GRP * STEPS * CAP
    row = lax.broadcasted_iota(jnp.int32, (n, n), 0)
    col = lax.broadcasted_iota(jnp.int32, (n, n), 1)
    wanted = ((row >> 1) & 3) * 8 + (row >> 3) * 2 + (row & 1)
    order = jnp.where(col == wanted, 1.0, 0.0).astype(jnp.bfloat16)
    arranged = jnp.dot(
        order, drecv[...].reshape(n, CH).astype(jnp.bfloat16), preferred_element_type=jnp.float32)
    dec_out[...] = arranged.reshape(STEPS, N_GRP * CAP, CH).astype(jnp.bfloat16)


def body(
    prompt_embed, prompt_lengths, decode_group, step_embed, norm_gain, w_query, w_key, w_value, w_out,
):
    smem = pl.BlockSpec(memory_space=pltpu.SMEM)
    vmem = pl.BlockSpec(memory_space=pltpu.VMEM)
    hbm = pl.BlockSpec(memory_space=pl.ANY)
    bf16, f32 = jnp.bfloat16, jnp.float32
    dma = pltpu.SemaphoreType.DMA
    prefill, decode = pl.pallas_call(
        kernel,
        name="layers",
        out_shape=(
            jax.ShapeDtypeStruct((PTOK, CH), bf16),
            jax.ShapeDtypeStruct((STEPS, N_GRP * CAP, CH), bf16),
        ),
        in_specs=[smem, smem, vmem, vmem, vmem, hbm, hbm, hbm, hbm],
        out_specs=(vmem, vmem),
        scratch_shapes=[
            pltpu.VMEM((D, NQKV), bf16),
            pltpu.VMEM((HQ * HD, D), bf16),
            pltpu.VMEM((N_TP, ROWS, CH), bf16),
            pltpu.VMEM((N_TP, ROWS, CH), bf16),
            pltpu.VMEM((N_TP, ROWS, CH), bf16),
            pltpu.VMEM((ROWS, CH), bf16),
            pltpu.VMEM((RMAX, CH), f32),
            pltpu.VMEM((RMAX, NQKV), f32),
            pltpu.VMEM((RMAX, HD), f32),
            pltpu.VMEM((RMAX, HQ * HD), bf16),
            pltpu.VMEM((KEYS, HD), bf16),
            pltpu.VMEM((KEYS, HD), bf16),
            pltpu.VMEM((ROWS, HD), f32),
            pltpu.VMEM((ROWS, HD), f32),
            pltpu.VMEM((ROWS, KEYS), f32),
            pltpu.VMEM((N_GRP, STEPS * CAP, CH), f32),
            pltpu.VMEM((N_GRP, STEPS * CAP, CH), f32),
            dma((4, N_TP)),
            dma((NB, N_TP)),
            dma((NB, N_TP)),
            dma((NB, N_TP)),
            dma((NB, N_TP)),
            dma((NB, N_TP)),
            dma((N_GRP,)),
            dma((N_GRP,)),
        ],
        compiler_params=pltpu.CompilerParams(
            collective_id=0, has_side_effects=True, vmem_limit_bytes=48 << 20),
    )(
        prompt_lengths,
        decode_group.reshape(N_GRP, DOCS),
        prompt_embed,
        step_embed.reshape(STEPS * DOCS, CH),
        norm_gain,
        w_query[0],
        w_key[0],
        w_value[0],
        w_out[0],
    )
    return prefill[None], decode[None]


def solution(mesh):
    return jax.shard_map(
        body,
        mesh=mesh,
        in_specs=(
            P("grp", "tp"),
            P(),
            P(),
            P(None, "grp", "tp"),
            P("phase", None),
            P("phase", None, "tp"),
            P("phase", None, "tp"),
            P("phase", None, "tp"),
            P("phase", "tp", None),
        ),
        out_specs=(P("phase", "grp", "tp"), P("phase", None, "grp", "tp")),
        check_vma=False,
    )
```

```python
import functools
import math

import jax
import jax.numpy as jnp
from jax import lax
from jax.experimental import pallas as pl
from jax.experimental.pallas import tpu as pltpu
from jax.sharding import PartitionSpec as P

D = 8192
HQ = 4
HD = 128
STEPS = 4
DOCS = 4
CAP = 2
N_TP = 8
N_GRP = 4
N_PHASE = 4
PTOK = 128
ROWS = PTOK + STEPS * DOCS
CH = D // N_TP
NQKV = (HQ + 2) * HD
KEYS = 256
EPS = 1e-06
THETA = 1000000.0
MESH = pl.DeviceIdType.MESH

R = 16
NB = ROWS // R
SLOTS = N_TP - 1
PASS_ON_AT = 2
FINISH_AT = 7
SLOT_FROM = ((0, 0), (1, 2), (0, 1), (1, 3), (0, 3), (1, 1), (1, 0), (0, 2))
NEIGHBOURS = ((0, 3), (0, 1), (1, 0))


def kernel(
    lens_hbm, dest_hbm, x_hbm, steps_hbm, gain_hbm, wq_hbm, wk_hbm, wv_hbm, wo_hbm,
    pre_out, dec_out,
    lens_ref, dest_ref, steps_ref, gain_ref, w, wo, xg, rs, st, xo, own, choice, kb, vb, cosb, sinb, bias,
    dsend, drecv,
    small_sem, wsem, first_send, next_send, hand_recv, ag_send, ag_recv, rs_send, rs_recv, dec_send, dec_recv,
):
    phase = lax.axis_index("phase")
    grp = lax.axis_index("grp")
    me = lax.axis_index("tp")
    my_y, my_z = me % 4, me // 4

    def at(row, along):
        return ((my_z + row) % 2) * 4 + (my_y + along) % 4

    def target(m):
        return at(1 - m // 4, 7 - m)

    opposite = at(1, 2)

    def slot(m, count=1):
        return pl.ds(m * CH, count * CH)

    def weight_copies(m):
        came = at(*SLOT_FROM[m])
        rows = pl.ds(came * CH, CH)
        return (
            pltpu.make_async_copy(wq_hbm.at[rows], w.at[slot(m), pl.ds(0, HQ * HD)], wsem.at[0, m]),
            pltpu.make_async_copy(wk_hbm.at[rows], w.at[slot(m), pl.ds(HQ * HD, HD)], wsem.at[1, m]),
            pltpu.make_async_copy(wv_hbm.at[rows], w.at[slot(m), pl.ds(HQ * HD + HD, HD)], wsem.at[2, m]),
            pltpu.make_async_copy(
                gain_hbm.at[:, pl.ds(pl.multiple_of(came * CH, CH), CH)], gain_ref.at[:, slot(m)], wsem.at[4, m]),
        )

    def out_weight_copy(m):
        cols = pl.ds(pl.multiple_of(target(m) * CH, CH), CH)
        return pltpu.make_async_copy(wo_hbm.at[:, cols], wo.at[:, slot(m)], wsem.at[3, m])

    barrier = pltpu.get_barrier_semaphore()

    def greet(device):
        pl.semaphore_signal(barrier, inc=1, device_id=device, device_id_type=MESH)

    for m in range(SLOTS):
        greet((phase, grp, target(m)))
    for k in range(1, N_GRP):
        greet((phase, (grp + k) % N_GRP, me))

    @pl.when(phase > 0)
    def _():
        greet((phase - 1, grp, me))
        greet((phase - 1, grp, opposite))

    @pl.when(phase < N_PHASE - 1)
    def _():
        greet((phase + 1, grp, me))
        greet((phase + 1, grp, opposite))

    small = [
        pltpu.make_async_copy(src, dst, small_sem.at[i])
        for i, (src, dst) in enumerate(((lens_hbm, lens_ref), (dest_hbm, dest_ref), (steps_hbm, steps_ref)))
    ]
    own_rows = pltpu.make_async_copy(x_hbm, xg.at[pl.ds(0, PTOK), slot(0)], small_sem.at[3])

    @pl.when(phase == 0)
    def _():
        own_rows.start()

    for copy in small:
        copy.start()
    for m in range(N_TP):
        for copy in weight_copies(m):
            copy.start()
    for m in range(N_TP):
        out_weight_copy(m).start()

    ahead = 1 + (phase == 0).astype(jnp.int32)

    def block(b):
        return pl.ds(pl.multiple_of(b * R, R), R)

    def first_copy(b):
        return pltpu.make_async_remote_copy(
            src_ref=xg.at[block(b), slot(0)], dst_ref=xg.at[block(b), slot(1)],
            send_sem=first_send, recv_sem=hand_recv.at[b, 1],
            device_id=(0, grp, opposite), device_id_type=MESH)

    def first_direct(m):
        row, along = SLOT_FROM[m]
        return pltpu.make_async_remote_copy(
            src_ref=xg.at[block(0), slot(0)], dst_ref=xg.at[block(0), slot(m)],
            send_sem=first_send, recv_sem=hand_recv.at[0, 1] if m == 1 else ag_recv.at[0, m // 2 - 1],
            device_id=(0, grp, at(row, 4 - along)), device_id_type=MESH)

    def next_copy(b, m):
        return pltpu.make_async_remote_copy(
            src_ref=xo.at[block(b)], dst_ref=xg.at[block(b), slot(m)],
            send_sem=next_send, recv_sem=hand_recv.at[b, m],
            device_id=(phase + 1, grp, (me, opposite)[m]), device_id_type=MESH)

    def forward_copy(b, n):
        return pltpu.make_async_remote_copy(
            src_ref=xg.at[block(b), slot(0, 2)], dst_ref=xg.at[block(b), slot(2 * n + 2, 2)],
            send_sem=ag_send, recv_sem=ag_recv.at[b, n],
            device_id=(phase, grp, at(*NEIGHBOURS[n])), device_id_type=MESH)

    def part_copy(b, m):
        return pltpu.make_async_remote_copy(
            src_ref=st.at[m, block(b)], dst_ref=rs.at[m, block(b)],
            send_sem=rs_send, recv_sem=rs_recv.at[b],
            device_id=(phase, grp, target(m)), device_id_type=MESH)

    def waiter(buffer, send_sem, recv_sem):
        return pltpu.make_async_remote_copy(
            src_ref=buffer, dst_ref=buffer, send_sem=send_sem, recv_sem=recv_sem,
            device_id=(phase, grp, target(0)), device_id_type=MESH)

    def forward(b):
        pl.when(phase > 0)(waiter(xg.at[block(b), slot(0)], rs_send, hand_recv.at[b, 0]).wait_recv)
        waiter(xg.at[block(b), slot(1)], rs_send, hand_recv.at[b, 1]).wait_recv()

        @pl.when((phase > 0) | (b > 0))
        def _():
            for n in range(len(NEIGHBOURS)):
                forward_copy(b, n).start()

    middle = ((phase > 0) & (phase < N_PHASE - 1)).astype(jnp.int32)
    pl.semaphore_wait(barrier, SLOTS + N_GRP - 1 + 2 + 2 * middle)
    for copy in small:
        copy.wait()

    @pl.when(phase == 0)
    def _():
        own_rows.wait()
        xg[PTOK:ROWS, 0:CH] = jnp.concatenate(
            [steps_ref[j].astype(jnp.float32) for j in range(STEPS)], axis=0).astype(jnp.bfloat16)

        for m in (5, 3, 7, 1, 4, 2, 6):
            first_direct(m).start()

        @pl.loop(1, NB)
        def _(b):
            first_copy(b).start()

    lens = [lens_ref[grp, d] for d in range(DOCS)]
    starts = [jnp.int32(0)]
    for d in range(DOCS):
        starts.append(starts[-1] + lens[d])

    def pick(values, index):
        out = jnp.full(index.shape, values[-1], jnp.int32)
        for d in range(DOCS - 1):
            out = jnp.where(index == d, values[d], out)
        return out

    def segment_and_place(row):
        of_prompt = sum((row >= starts[d]).astype(jnp.int32) for d in range(1, DOCS))
        of_step = (row - PTOK) & (DOCS - 1)
        step = (row - PTOK) >> 2
        segment = jnp.where(row < PTOK, of_prompt, of_step)
        place = jnp.where(row < PTOK, row - pick(starts[:DOCS], of_prompt), pick(lens, of_step) + step)
        return jnp.where(row < ROWS, segment, -1), place

    seg_q, place_q = segment_and_place(lax.broadcasted_iota(jnp.int32, (ROWS, HD), 0))
    lane = lax.broadcasted_iota(jnp.int32, (ROWS, HD), 1)
    half = (lane & (HD // 2 - 1)).astype(jnp.float32)
    angle = place_q.astype(jnp.float32) * jnp.exp(half * (-2.0 / HD * math.log(THETA)))
    cosb[...] = jnp.cos(angle)
    sine = jnp.sin(angle)
    sinb[...] = jnp.where(lane < HD // 2, -sine, sine)
    for part in range(KEYS // HD):
        seg_k, place_k = segment_and_place(lax.broadcasted_iota(jnp.int32, (ROWS, HD), 1) + part * HD)
        bias[:, part * HD : (part + 1) * HD] = jnp.where((seg_q == seg_k) & (place_k <= place_q), 0.0, -1e30)
    row = lax.broadcasted_iota(jnp.int32, (N_GRP * STEPS * CAP, STEPS * DOCS), 0)
    col = lax.broadcasted_iota(jnp.int32, (N_GRP * STEPS * CAP, STEPS * DOCS), 1)
    dests = [dest_ref[grp, d] for d in range(DOCS)]
    ranks = [
        sum([(dests[e] == dests[d]).astype(jnp.int32) for e in range(d)], jnp.int32(0)) for d in range(DOCS)
    ]
    doc = col & (DOCS - 1)
    chosen = (
        (pick(dests, doc) == (row >> 3)) & (pick(ranks, doc) == (row & 1)) & ((col >> 2) == ((row >> 1) & 3))
    )
    choice[...] = jnp.where(chosen, 1.0, 0.0).astype(jnp.bfloat16)
    kb[...] = jnp.zeros_like(kb)
    vb[:, 0:HD] = jnp.zeros((KEYS, HD), jnp.bfloat16)
    vb[:, HD:] = jnp.ones((KEYS, HD), jnp.bfloat16)
    for m in range(N_TP):
        for copy in weight_copies(m):
            copy.wait()

    def project_in(b):
        def pass_on():
            @pl.when(b < NB - ahead)
            def _():
                forward(b + ahead)

        total, squared = None, None
        for m in range(N_TP):
            if m == PASS_ON_AT:
                pass_on()
            if m > 1 and m % 2 == 0:
                waiter(xg.at[block(b), slot(m, 2)], rs_send, ag_recv.at[b, m // 2 - 1]).wait_recv()
            values = xg[block(b), m * CH : (m + 1) * CH].astype(jnp.float32)
            squares = values * values
            piece = sum(squares[:, i * HD : (i + 1) * HD] for i in range(CH // HD))
            scaled = (values * gain_ref[:, m * CH : (m + 1) * CH]).astype(jnp.bfloat16)
            product = jnp.dot(scaled, w[m * CH : (m + 1) * CH, :], preferred_element_type=jnp.float32)
            total = product if total is None else total + product
            squared = piece if squared is None else squared + piece
        return total * lax.rsqrt(jnp.sum(squared, axis=-1, keepdims=True) * (1.0 / D) + EPS)

    def attend(b, projected):
        cosine, sine = cosb[block(b)], sinb[block(b)]

        def rotated(values):
            return (values * cosine + pltpu.roll(values, HD // 2, 1) * sine).astype(jnp.bfloat16)

        heads = [rotated(projected[:, h * HD : (h + 1) * HD]) for h in range(HQ + 1)]
        kb[block(b)] = heads[HQ]
        vb[block(b), 0:HD] = projected[:, (HQ + 1) * HD :].astype(jnp.bfloat16)
        queries = jnp.concatenate(heads[:HQ], axis=0)
        scores = lax.dot_general(
            queries, kb[...], (((1,), (1,)), ((), ())), preferred_element_type=jnp.float32)
        scores = scores * (1.0 / math.sqrt(HD)) + jnp.concatenate([bias[block(b)]] * HQ, axis=0)
        raised = jnp.exp(scores - jnp.max(scores, axis=-1, keepdims=True)).astype(jnp.bfloat16)
        mixed = jnp.dot(raised, vb[...], preferred_element_type=jnp.float32)
        mixed = (mixed[:, 0:HD] / mixed[:, HD:]).astype(jnp.bfloat16)
        return jnp.concatenate([mixed[h * R : (h + 1) * R] for h in range(HQ)], axis=1)

    def finish(b):
        waiter(rs.at[:, block(b)], rs_send, rs_recv.at[b]).wait_recv()
        total = own[b % 2] + xg[block(b), 0:CH].astype(jnp.float32)
        for m in range(SLOTS):
            total += rs[m, block(b)].astype(jnp.float32)
        xo[block(b)] = total.astype(jnp.bfloat16)

        @pl.when(phase < N_PHASE - 1)
        def _():
            next_copy(b, 1).start()
            next_copy(b, 0).start()

    def project_out(b, heads):
        def product(m):
            return jnp.dot(heads, wo[:, m * CH : (m + 1) * CH], preferred_element_type=jnp.float32)

        ready = product(0)
        for m in range(SLOTS):
            if m == FINISH_AT:
                pl.when(b > 0)(functools.partial(finish, b - 1))
            following = product(m + 1)
            st[m, block(b)] = ready.astype(jnp.bfloat16)
            part_copy(b, m).start()
            ready = following
        own[b % 2] = ready
        if FINISH_AT == SLOTS:
            pl.when(b > 0)(functools.partial(finish, b - 1))

    forward(0)

    @pl.when(phase == 0)
    def _():
        forward(1)

    @pl.loop(0, NB)
    def _(b):

        projected = project_in(b)
        heads = attend(b, projected)

        @pl.when(b == 0)
        def _():
            for m in range(N_TP):
                out_weight_copy(m).wait()

        project_out(b, heads)


    finish(NB - 1)

    picked = jnp.dot(choice[...], xo[PTOK:ROWS], preferred_element_type=jnp.float32)
    for g in range(N_GRP):
        rows = picked[g * STEPS * CAP : (g + 1) * STEPS * CAP]
        dsend[g] = jnp.concatenate([rows[:, : CH // 2], rows[:, CH // 2 :]], axis=0).astype(jnp.bfloat16)

    def decode_copy(k):
        to = (grp + k) % N_GRP
        return pltpu.make_async_remote_copy(
            src_ref=dsend.at[to], dst_ref=drecv.at[grp],
            send_sem=dec_send.at[k], recv_sem=dec_recv.at[k],
            device_id=(phase, to, me), device_id_type=MESH)

    for k in range(1, N_GRP):
        decode_copy(k).start()
    drecv[grp] = dsend[grp]
    pre_out[...] = xo[0:PTOK]

    @pl.when(phase == 0)
    def _():
        waiter(xg.at[:, slot(0)], first_send, rs_recv.at[0]).wait_send()
        waiter(xg.at[block(0), slot(0, 6)], first_send, rs_recv.at[0]).wait_send()
        waiter(xg.at[pl.ds(R, ROWS - R), slot(0, 6)], ag_send, rs_recv.at[0]).wait_send()

    @pl.when(phase < N_PHASE - 1)
    def _():
        waiter(xg.at[:, slot(0, 2)], next_send, rs_recv.at[0]).wait_send()

    @pl.when(phase > 0)
    def _():
        waiter(xg.at[:, slot(0, 6)], ag_send, rs_recv.at[0]).wait_send()

    waiter(st, rs_send, rs_recv.at[0]).wait_send()

    for k in range(1, N_GRP):
        came = (grp + N_GRP - k) % N_GRP
        pltpu.make_async_remote_copy(
            src_ref=dsend.at[came], dst_ref=drecv.at[came],
            send_sem=dec_send.at[k], recv_sem=dec_recv.at[k],
            device_id=(phase, came, me), device_id_type=MESH).wait_recv()
        decode_copy(k).wait_send()
    n = N_GRP * STEPS * CAP
    row = lax.broadcasted_iota(jnp.int32, (n, 2 * n), 0)
    col = lax.broadcasted_iota(jnp.int32, (n, 2 * n), 1)
    wanted = ((row >> 1) & 3) * 16 + (row >> 3) * 2 + (row & 1)
    received = drecv[...].reshape(2 * n, CH // 2)
    for part in range(2):
        order = jnp.where(col == wanted + part * STEPS * CAP, 1.0, 0.0).astype(jnp.bfloat16)
        arranged = jnp.dot(order, received, preferred_element_type=jnp.float32)
        dec_out[:, :, part * (CH // 2) : (part + 1) * (CH // 2)] = arranged.reshape(
            STEPS, N_GRP * CAP, CH // 2).astype(jnp.bfloat16)


def body(
    prompt_embed, prompt_lengths, decode_group, step_embed, norm_gain, w_query, w_key, w_value, w_out,
):
    vmem = pl.BlockSpec(memory_space=pltpu.VMEM)
    hbm = pl.BlockSpec(memory_space=pl.ANY)
    bf16, f32 = jnp.bfloat16, jnp.float32
    dma = pltpu.SemaphoreType.DMA
    prefill, decode = pl.pallas_call(
        kernel,
        name="layers",
        out_shape=(
            jax.ShapeDtypeStruct((PTOK, CH), bf16),
            jax.ShapeDtypeStruct((STEPS, N_GRP * CAP, CH), bf16),
        ),
        in_specs=[hbm] * 9,
        out_specs=(vmem, vmem),
        scratch_shapes=[
            pltpu.SMEM((N_GRP, DOCS), jnp.int32),
            pltpu.SMEM((N_GRP, DOCS), jnp.int32),
            pltpu.VMEM((STEPS, DOCS, CH), bf16),
            pltpu.VMEM((1, D), f32),
            pltpu.VMEM((D, NQKV), bf16),
            pltpu.VMEM((HQ * HD, D), bf16),
            pltpu.VMEM((ROWS, D), bf16),
            pltpu.VMEM((SLOTS, ROWS, CH), bf16),
            pltpu.VMEM((SLOTS, ROWS, CH), bf16),
            pltpu.VMEM((ROWS, CH), bf16),
            pltpu.VMEM((2, R, CH), f32),
            pltpu.VMEM((N_GRP * STEPS * CAP, STEPS * DOCS), bf16),
            pltpu.VMEM((KEYS, HD), bf16),
            pltpu.VMEM((KEYS, 2 * HD), bf16),
            pltpu.VMEM((ROWS, HD), f32),
            pltpu.VMEM((ROWS, HD), f32),
            pltpu.VMEM((ROWS, KEYS), f32),
            pltpu.VMEM((N_GRP, 2 * STEPS * CAP, CH // 2), bf16),
            pltpu.VMEM((N_GRP, 2 * STEPS * CAP, CH // 2), bf16),
            dma((4,)),
            dma((5, N_TP)),
            dma(()),
            dma(()),
            dma((NB, 2)),
            dma(()),
            dma((NB, len(NEIGHBOURS))),
            dma(()),
            dma((NB,)),
            dma((N_GRP,)),
            dma((N_GRP,)),
        ],
        compiler_params=pltpu.CompilerParams(
            collective_id=0, has_side_effects=True, vmem_limit_bytes=60 << 20),
    )(
        prompt_lengths,
        decode_group.reshape(N_GRP, DOCS),
        prompt_embed,
        step_embed,
        norm_gain,
        w_query[0],
        w_key[0],
        w_value[0],
        w_out[0],
    )
    return prefill[None], decode[None]


def solution(mesh):
    return jax.shard_map(
        body,
        mesh=mesh,
        in_specs=(
            P("grp", "tp"),
            P(),
            P(),
            P(None, "grp", "tp"),
            P("phase", None),
            P("phase", None, "tp"),
            P("phase", None, "tp"),
            P("phase", None, "tp"),
            P("phase", "tp", None),
        ),
        out_specs=(P("phase", "grp", "tp"), P("phase", None, "grp", "tp")),
        check_vma=False,
    )
```

```python
import functools
import math

import jax
import jax.numpy as jnp
from jax import lax
from jax.experimental import pallas as pl
from jax.experimental.pallas import tpu as pltpu
from jax.sharding import PartitionSpec as P

D = 8192
HQ = 4
HD = 128
STEPS = 4
DOCS = 4
CAP = 2
N_TP = 8
N_GRP = 4
N_PHASE = 4
PTOK = 128
ROWS = PTOK + STEPS * DOCS
CH = D // N_TP
NQKV = (HQ + 2) * HD
KEYS = 256
EPS = 1e-06
THETA = 1000000.0
MESH = pl.DeviceIdType.MESH

R = 16
NB = ROWS // R
SLOTS = N_TP - 1
SHARE_TO = ((1, 2), (1, 1), (1, 3), (0, 2), (1, 0), (0, 1), (0, 3), (0, 0))
PASS_ON_AT = 2
SLOT_FROM = ((0, 0), (1, 2), (0, 1), (1, 3), (0, 3), (1, 1), (1, 0), (0, 2))
NEIGHBOURS = ((0, 3), (0, 1), (1, 0))


def kernel(
    lens_hbm, dest_hbm, x_hbm, steps_hbm, gain_hbm, wq_hbm, wk_hbm, wv_hbm, wo_hbm,
    pre_out, dec_out,
    lens_ref, dest_ref, steps_ref, gain_ref, w, wo, xg, rs, st, xo, own, choice, kb, vb, cosb, sinb, bias,
    dsend, drecv,
    small_sem, wsem, first_send, next_send, hand_recv, ag_send, ag_recv, rs_send, rs_recv, dec_send, dec_recv,
):
    phase = lax.axis_index("phase")
    grp = lax.axis_index("grp")
    me = lax.axis_index("tp")
    my_y, my_z = me % 4, me // 4

    def at(row, along):
        return ((my_z + row) % 2) * 4 + (my_y + along) % 4

    def target(m):
        return at(*SHARE_TO[m])

    opposite = at(1, 2)

    def slot(m, count=1):
        return pl.ds(m * CH, count * CH)

    def weight_copies(m):
        came = at(*SLOT_FROM[m])
        rows = pl.ds(came * CH, CH)
        return (
            pltpu.make_async_copy(wq_hbm.at[rows], w.at[slot(m), pl.ds(0, HQ * HD)], wsem.at[0, m]),
            pltpu.make_async_copy(wk_hbm.at[rows], w.at[slot(m), pl.ds(HQ * HD, HD)], wsem.at[1, m]),
            pltpu.make_async_copy(wv_hbm.at[rows], w.at[slot(m), pl.ds(HQ * HD + HD, HD)], wsem.at[2, m]),
            pltpu.make_async_copy(
                gain_hbm.at[:, pl.ds(pl.multiple_of(came * CH, CH), CH)], gain_ref.at[:, slot(m)], wsem.at[4, m]),
        )

    def out_weight_copy(m):
        cols = pl.ds(pl.multiple_of(target(m) * CH, CH), CH)
        return pltpu.make_async_copy(wo_hbm.at[:, cols], wo.at[:, slot(m)], wsem.at[3, m])

    barrier = pltpu.get_barrier_semaphore()

    def greet(device):
        pl.semaphore_signal(barrier, inc=1, device_id=device, device_id_type=MESH)

    for m in range(SLOTS):
        greet((phase, grp, target(m)))
    for k in range(1, N_GRP):
        greet((phase, (grp + k) % N_GRP, me))

    @pl.when(phase > 0)
    def _():
        greet((phase - 1, grp, me))
        greet((phase - 1, grp, opposite))

    @pl.when(phase < N_PHASE - 1)
    def _():
        greet((phase + 1, grp, me))
        greet((phase + 1, grp, opposite))

    small = [
        pltpu.make_async_copy(src, dst, small_sem.at[i])
        for i, (src, dst) in enumerate(((lens_hbm, lens_ref), (dest_hbm, dest_ref), (steps_hbm, steps_ref)))
    ]
    own_rows = pltpu.make_async_copy(x_hbm, xg.at[pl.ds(0, PTOK), slot(0)], small_sem.at[3])

    @pl.when(phase == 0)
    def _():
        own_rows.start()

    for copy in small:
        copy.start()
    for m in range(N_TP):
        for copy in weight_copies(m):
            copy.start()
    for m in range(N_TP):
        out_weight_copy(m).start()

    ahead = 1 + (phase == 0).astype(jnp.int32)

    def block(b):
        return pl.ds(pl.multiple_of(b * R, R), R)

    def first_copy(b):
        return pltpu.make_async_remote_copy(
            src_ref=xg.at[block(b), slot(0)], dst_ref=xg.at[block(b), slot(1)],
            send_sem=first_send, recv_sem=hand_recv.at[b, 1],
            device_id=(0, grp, opposite), device_id_type=MESH)

    def first_direct(m):
        row, along = SLOT_FROM[m]
        return pltpu.make_async_remote_copy(
            src_ref=xg.at[block(0), slot(0)], dst_ref=xg.at[block(0), slot(m)],
            send_sem=first_send, recv_sem=hand_recv.at[0, 1] if m == 1 else ag_recv.at[0, m // 2 - 1],
            device_id=(0, grp, at(row, 4 - along)), device_id_type=MESH)

    def next_copy(b, m):
        return pltpu.make_async_remote_copy(
            src_ref=xo.at[block(b)], dst_ref=xg.at[block(b), slot(m)],
            send_sem=next_send, recv_sem=hand_recv.at[b, m],
            device_id=(phase + 1, grp, (me, opposite)[m]), device_id_type=MESH)

    def forward_copy(b, n):
        return pltpu.make_async_remote_copy(
            src_ref=xg.at[block(b), slot(0, 2)], dst_ref=xg.at[block(b), slot(2 * n + 2, 2)],
            send_sem=ag_send, recv_sem=ag_recv.at[b, n],
            device_id=(phase, grp, at(*NEIGHBOURS[n])), device_id_type=MESH)

    def part_copy(b, m):
        return pltpu.make_async_remote_copy(
            src_ref=st.at[m, block(b)], dst_ref=rs.at[m, block(b)],
            send_sem=rs_send, recv_sem=rs_recv.at[b],
            device_id=(phase, grp, target(m)), device_id_type=MESH)

    def waiter(buffer, send_sem, recv_sem):
        return pltpu.make_async_remote_copy(
            src_ref=buffer, dst_ref=buffer, send_sem=send_sem, recv_sem=recv_sem,
            device_id=(phase, grp, target(0)), device_id_type=MESH)

    def forward(b):
        pl.when(phase > 0)(waiter(xg.at[block(b), slot(0)], rs_send, hand_recv.at[b, 0]).wait_recv)
        waiter(xg.at[block(b), slot(1)], rs_send, hand_recv.at[b, 1]).wait_recv()

        @pl.when((phase > 0) | (b > 0))
        def _():
            for n in range(len(NEIGHBOURS)):
                forward_copy(b, n).start()

    middle = ((phase > 0) & (phase < N_PHASE - 1)).astype(jnp.int32)
    pl.semaphore_wait(barrier, SLOTS + N_GRP - 1 + 2 + 2 * middle)
    for copy in small:
        copy.wait()

    @pl.when(phase == 0)
    def _():
        own_rows.wait()
        xg[PTOK:ROWS, 0:CH] = jnp.concatenate(
            [steps_ref[j].astype(jnp.float32) for j in range(STEPS)], axis=0).astype(jnp.bfloat16)

        for m in (5, 3, 7, 1, 4, 2, 6):
            first_direct(m).start()

        @pl.loop(1, NB)
        def _(b):
            first_copy(b).start()

    lens = [lens_ref[grp, d] for d in range(DOCS)]
    starts = [jnp.int32(0)]
    for d in range(DOCS):
        starts.append(starts[-1] + lens[d])

    def pick(values, index):
        out = jnp.full(index.shape, values[-1], jnp.int32)
        for d in range(DOCS - 1):
            out = jnp.where(index == d, values[d], out)
        return out

    def segment_and_place(row):
        of_prompt = sum((row >= starts[d]).astype(jnp.int32) for d in range(1, DOCS))
        of_step = (row - PTOK) & (DOCS - 1)
        step = (row - PTOK) >> 2
        segment = jnp.where(row < PTOK, of_prompt, of_step)
        place = jnp.where(row < PTOK, row - pick(starts[:DOCS], of_prompt), pick(lens, of_step) + step)
        return jnp.where(row < ROWS, segment, -1), place

    seg_q, place_q = segment_and_place(lax.broadcasted_iota(jnp.int32, (ROWS, HD), 0))
    lane = lax.broadcasted_iota(jnp.int32, (ROWS, HD), 1)
    half = (lane & (HD // 2 - 1)).astype(jnp.float32)
    angle = place_q.astype(jnp.float32) * jnp.exp(half * (-2.0 / HD * math.log(THETA)))
    cosb[...] = jnp.cos(angle)
    sine = jnp.sin(angle)
    sinb[...] = jnp.where(lane < HD // 2, -sine, sine)
    for part in range(KEYS // HD):
        seg_k, place_k = segment_and_place(lax.broadcasted_iota(jnp.int32, (ROWS, HD), 1) + part * HD)
        bias[:, part * HD : (part + 1) * HD] = jnp.where((seg_q == seg_k) & (place_k <= place_q), 0.0, -1e30)
    row = lax.broadcasted_iota(jnp.int32, (N_GRP * STEPS * CAP, STEPS * DOCS), 0)
    col = lax.broadcasted_iota(jnp.int32, (N_GRP * STEPS * CAP, STEPS * DOCS), 1)
    dests = [dest_ref[grp, d] for d in range(DOCS)]
    ranks = [
        sum([(dests[e] == dests[d]).astype(jnp.int32) for e in range(d)], jnp.int32(0)) for d in range(DOCS)
    ]
    doc = col & (DOCS - 1)
    chosen = (
        (pick(dests, doc) == (row >> 3)) & (pick(ranks, doc) == (row & 1)) & ((col >> 2) == ((row >> 1) & 3))
    )
    choice[...] = jnp.where(chosen, 1.0, 0.0).astype(jnp.bfloat16)
    kb[...] = jnp.zeros_like(kb)
    vb[:, 0:HD] = jnp.zeros((KEYS, HD), jnp.bfloat16)
    vb[:, HD:] = jnp.ones((KEYS, HD), jnp.bfloat16)
    for m in range(N_TP):
        for copy in weight_copies(m):
            copy.wait()

    def project_in(b):
        def pass_on():
            @pl.when(b < NB - ahead)
            def _():
                forward(b + ahead)

        total, squared = None, None
        for m in range(N_TP):
            if m == PASS_ON_AT:
                pass_on()
            if m > 1 and m % 2 == 0:
                waiter(xg.at[block(b), slot(m, 2)], rs_send, ag_recv.at[b, m // 2 - 1]).wait_recv()
            values = xg[block(b), m * CH : (m + 1) * CH].astype(jnp.float32)
            squares = values * values
            piece = sum(squares[:, i * HD : (i + 1) * HD] for i in range(CH // HD))
            scaled = (values * gain_ref[:, m * CH : (m + 1) * CH]).astype(jnp.bfloat16)
            product = jnp.dot(scaled, w[m * CH : (m + 1) * CH, :], preferred_element_type=jnp.float32)
            total = product if total is None else total + product
            squared = piece if squared is None else squared + piece
        return total * lax.rsqrt(jnp.sum(squared, axis=-1, keepdims=True) * (1.0 / D) + EPS)

    def attend(b, projected):
        cosine, sine = cosb[block(b)], sinb[block(b)]

        def rotated(values):
            return (values * cosine + pltpu.roll(values, HD // 2, 1) * sine).astype(jnp.bfloat16)

        heads = [rotated(projected[:, h * HD : (h + 1) * HD]) for h in range(HQ + 1)]
        kb[block(b)] = heads[HQ]
        vb[block(b), 0:HD] = projected[:, (HQ + 1) * HD :].astype(jnp.bfloat16)
        queries = jnp.concatenate(heads[:HQ], axis=0)
        scores = lax.dot_general(
            queries, kb[...], (((1,), (1,)), ((), ())), preferred_element_type=jnp.float32)
        scores = scores * (1.0 / math.sqrt(HD)) + jnp.concatenate([bias[block(b)]] * HQ, axis=0)
        raised = jnp.exp(scores - jnp.max(scores, axis=-1, keepdims=True)).astype(jnp.bfloat16)
        mixed = jnp.dot(raised, vb[...], preferred_element_type=jnp.float32)
        mixed = (mixed[:, 0:HD] / mixed[:, HD:]).astype(jnp.bfloat16)
        return jnp.concatenate([mixed[h * R : (h + 1) * R] for h in range(HQ)], axis=1)

    def finish(b):
        waiter(rs.at[:, block(b)], rs_send, rs_recv.at[b]).wait_recv()
        total = own[b % 2]
        for m in range(SLOTS):
            total += rs[m, block(b)].astype(jnp.float32)
        xo[block(b)] = total.astype(jnp.bfloat16)

        @pl.when(phase < N_PHASE - 1)
        def _():
            next_copy(b, 1).start()
            next_copy(b, 0).start()

    def project_out(b, heads):
        def product(m):
            return jnp.dot(heads, wo[:, m * CH : (m + 1) * CH], preferred_element_type=jnp.float32)

        ready = product(0)
        for m in range(SLOTS):
            following = product(m + 1)
            st[m, block(b)] = ready.astype(jnp.bfloat16)
            part_copy(b, m).start()
            ready = following
        own[b % 2] = ready + xg[block(b), 0:CH].astype(jnp.float32)

    forward(0)

    @pl.when(phase == 0)
    def _():
        forward(1)

    @pl.loop(0, NB)
    def _(b):

        projected = project_in(b)
        heads = attend(b, projected)

        @pl.when(b == 0)
        def _():
            for m in range(N_TP):
                out_weight_copy(m).wait()

        project_out(b, heads)
        pl.when(b > 0)(functools.partial(finish, b - 1))


    finish(NB - 1)

    picked = jnp.dot(choice[...], xo[PTOK:ROWS], preferred_element_type=jnp.float32)
    for g in range(N_GRP):
        rows = picked[g * STEPS * CAP : (g + 1) * STEPS * CAP]
        dsend[g] = jnp.concatenate([rows[:, : CH // 2], rows[:, CH // 2 :]], axis=0).astype(jnp.bfloat16)

    def decode_copy(k):
        to = (grp + k) % N_GRP
        return pltpu.make_async_remote_copy(
            src_ref=dsend.at[to], dst_ref=drecv.at[grp],
            send_sem=dec_send.at[k], recv_sem=dec_recv.at[k],
            device_id=(phase, to, me), device_id_type=MESH)

    for k in range(1, N_GRP):
        decode_copy(k).start()
    n = N_GRP * STEPS * CAP
    row = lax.broadcasted_iota(jnp.int32, (n, 2 * n), 0)
    col = lax.broadcasted_iota(jnp.int32, (n, 2 * n), 1)
    wanted = ((row >> 1) & 3) * 16 + (row >> 3) * 2 + (row & 1)
    orders = [jnp.where(col == wanted + part * STEPS * CAP, 1.0, 0.0).astype(jnp.bfloat16) for part in range(2)]
    drecv[grp] = dsend[grp]
    pre_out[...] = xo[0:PTOK]

    @pl.when(phase == 0)
    def _():
        waiter(xg.at[:, slot(0)], first_send, rs_recv.at[0]).wait_send()
        waiter(xg.at[block(0), slot(0, 6)], first_send, rs_recv.at[0]).wait_send()
        waiter(xg.at[pl.ds(R, ROWS - R), slot(0, 6)], ag_send, rs_recv.at[0]).wait_send()

    @pl.when(phase < N_PHASE - 1)
    def _():
        waiter(xg.at[:, slot(0, 2)], next_send, rs_recv.at[0]).wait_send()

    @pl.when(phase > 0)
    def _():
        waiter(xg.at[:, slot(0, 6)], ag_send, rs_recv.at[0]).wait_send()

    waiter(st, rs_send, rs_recv.at[0]).wait_send()

    for k in range(1, N_GRP):
        came = (grp + N_GRP - k) % N_GRP
        pltpu.make_async_remote_copy(
            src_ref=dsend.at[came], dst_ref=drecv.at[came],
            send_sem=dec_send.at[k], recv_sem=dec_recv.at[k],
            device_id=(phase, came, me), device_id_type=MESH).wait_recv()
        decode_copy(k).wait_send()
    received = drecv[...].reshape(2 * n, CH // 2)
    for part in range(2):
        arranged = jnp.dot(orders[part], received, preferred_element_type=jnp.float32)
        dec_out[:, :, part * (CH // 2) : (part + 1) * (CH // 2)] = arranged.reshape(
            STEPS, N_GRP * CAP, CH // 2).astype(jnp.bfloat16)


def body(
    prompt_embed, prompt_lengths, decode_group, step_embed, norm_gain, w_query, w_key, w_value, w_out,
):
    vmem = pl.BlockSpec(memory_space=pltpu.VMEM)
    hbm = pl.BlockSpec(memory_space=pl.ANY)
    bf16, f32 = jnp.bfloat16, jnp.float32
    dma = pltpu.SemaphoreType.DMA
    prefill, decode = pl.pallas_call(
        kernel,
        name="layers",
        out_shape=(
            jax.ShapeDtypeStruct((PTOK, CH), bf16),
            jax.ShapeDtypeStruct((STEPS, N_GRP * CAP, CH), bf16),
        ),
        in_specs=[hbm] * 9,
        out_specs=(vmem, vmem),
        scratch_shapes=[
            pltpu.SMEM((N_GRP, DOCS), jnp.int32),
            pltpu.SMEM((N_GRP, DOCS), jnp.int32),
            pltpu.VMEM((STEPS, DOCS, CH), bf16),
            pltpu.VMEM((1, D), f32),
            pltpu.VMEM((D, NQKV), bf16),
            pltpu.VMEM((HQ * HD, D), bf16),
            pltpu.VMEM((ROWS, D), bf16),
            pltpu.VMEM((SLOTS, ROWS, CH), bf16),
            pltpu.VMEM((SLOTS, ROWS, CH), bf16),
            pltpu.VMEM((ROWS, CH), bf16),
            pltpu.VMEM((2, R, CH), f32),
            pltpu.VMEM((N_GRP * STEPS * CAP, STEPS * DOCS), bf16),
            pltpu.VMEM((KEYS, HD), bf16),
            pltpu.VMEM((KEYS, 2 * HD), bf16),
            pltpu.VMEM((ROWS, HD), f32),
            pltpu.VMEM((ROWS, HD), f32),
            pltpu.VMEM((ROWS, KEYS), f32),
            pltpu.VMEM((N_GRP, 2 * STEPS * CAP, CH // 2), bf16),
            pltpu.VMEM((N_GRP, 2 * STEPS * CAP, CH // 2), bf16),
            dma((4,)),
            dma((5, N_TP)),
            dma(()),
            dma(()),
            dma((NB, 2)),
            dma(()),
            dma((NB, len(NEIGHBOURS))),
            dma(()),
            dma((NB,)),
            dma((N_GRP,)),
            dma((N_GRP,)),
        ],
        compiler_params=pltpu.CompilerParams(
            collective_id=0, has_side_effects=True, vmem_limit_bytes=60 << 20),
    )(
        prompt_lengths,
        decode_group.reshape(N_GRP, DOCS),
        prompt_embed,
        step_embed,
        norm_gain,
        w_query[0],
        w_key[0],
        w_value[0],
        w_out[0],
    )
    return prefill[None], decode[None]


def solution(mesh):
    return jax.shard_map(
        body,
        mesh=mesh,
        in_specs=(
            P("grp", "tp"),
            P(),
            P(),
            P(None, "grp", "tp"),
            P("phase", None),
            P("phase", None, "tp"),
            P("phase", None, "tp"),
            P("phase", None, "tp"),
            P("phase", "tp", None),
        ),
        out_specs=(P("phase", "grp", "tp"), P("phase", None, "grp", "tp")),
        check_vma=False,
    )
```

```python
import functools
import math

import jax
import jax.numpy as jnp
from jax import lax
from jax.experimental import pallas as pl
from jax.experimental.pallas import tpu as pltpu
from jax.sharding import PartitionSpec as P

D = 8192
HQ = 4
HD = 128
STEPS = 4
DOCS = 4
CAP = 2
N_TP = 8
N_GRP = 4
N_PHASE = 4
PTOK = 128
ROWS = PTOK + STEPS * DOCS
CH = D // N_TP
NQKV = (HQ + 2) * HD
KEYS = 256
EPS = 1e-06
THETA = 1000000.0
MESH = pl.DeviceIdType.MESH

R = 16
NB = ROWS // R
SLOTS = N_TP - 1
SHARE_TO = ((1, 2), (1, 1), (1, 3), (0, 2), (1, 0), (0, 1), (0, 3), (0, 0))
PASS_ON_AT = 2
SLOT_FROM = ((0, 0), (1, 2), (0, 1), (1, 3), (0, 3), (1, 1), (1, 0), (0, 2))
NEIGHBOURS = ((0, 3), (0, 1), (1, 0))


def kernel(
    lens_hbm, dest_hbm, x_hbm, steps_hbm, gain_hbm, wq_hbm, wk_hbm, wv_hbm, wo_hbm,
    pre_out, dec_out,
    lens_ref, dest_ref, steps_ref, gain_ref, w, wo, xg, rs, st, xo, own, choice, kb, vb, cosb, sinb, bias,
    dsend, drecv,
    small_sem, wsem, first_send, next_send, hand_recv, ag_send, ag_recv, rs_send, rs_recv, dec_send, dec_recv,
):
    phase = lax.axis_index("phase")
    grp = lax.axis_index("grp")
    me = lax.axis_index("tp")
    my_y, my_z = me % 4, me // 4

    def at(row, along):
        return ((my_z + row) % 2) * 4 + (my_y + along) % 4

    def target(m):
        return at(*SHARE_TO[m])

    opposite = at(1, 2)

    def slot(m, count=1):
        return pl.ds(m * CH, count * CH)

    def weight_copies(m):
        came = at(*SLOT_FROM[m])
        rows = pl.ds(came * CH, CH)
        return (
            pltpu.make_async_copy(wq_hbm.at[rows], w.at[slot(m), pl.ds(0, HQ * HD)], wsem.at[0, m]),
            pltpu.make_async_copy(wk_hbm.at[rows], w.at[slot(m), pl.ds(HQ * HD, HD)], wsem.at[1, m]),
            pltpu.make_async_copy(wv_hbm.at[rows], w.at[slot(m), pl.ds(HQ * HD + HD, HD)], wsem.at[2, m]),
            pltpu.make_async_copy(
                gain_hbm.at[:, pl.ds(pl.multiple_of(came * CH, CH), CH)], gain_ref.at[:, slot(m)], wsem.at[4, m]),
        )

    def out_weight_copy(m):
        cols = pl.ds(pl.multiple_of(target(m) * CH, CH), CH)
        return pltpu.make_async_copy(wo_hbm.at[:, cols], wo.at[:, slot(m)], wsem.at[3, m])

    barrier = pltpu.get_barrier_semaphore()

    def greet(device):
        pl.semaphore_signal(barrier, inc=1, device_id=device, device_id_type=MESH)

    for m in range(SLOTS):
        greet((phase, grp, target(m)))
    for k in range(1, N_GRP):
        greet((phase, (grp + k) % N_GRP, me))

    @pl.when(phase > 0)
    def _():
        greet((phase - 1, grp, me))
        greet((phase - 1, grp, opposite))

    @pl.when(phase < N_PHASE - 1)
    def _():
        greet((phase + 1, grp, me))
        greet((phase + 1, grp, opposite))

    small = [
        pltpu.make_async_copy(src, dst, small_sem.at[i])
        for i, (src, dst) in enumerate(((lens_hbm, lens_ref), (dest_hbm, dest_ref), (steps_hbm, steps_ref)))
    ]
    own_rows = pltpu.make_async_copy(x_hbm, xg.at[pl.ds(0, PTOK), slot(0)], small_sem.at[3])

    @pl.when(phase == 0)
    def _():
        own_rows.start()

    for copy in small:
        copy.start()
    for m in range(N_TP):
        for copy in weight_copies(m):
            copy.start()
    for m in range(N_TP):
        out_weight_copy(m).start()

    ahead = 1 + (phase == 0).astype(jnp.int32)

    def block(b):
        return pl.ds(pl.multiple_of(b * R, R), R)

    def first_copy(b):
        return pltpu.make_async_remote_copy(
            src_ref=xg.at[block(b), slot(0)], dst_ref=xg.at[block(b), slot(1)],
            send_sem=first_send, recv_sem=hand_recv.at[b, 1],
            device_id=(0, grp, opposite), device_id_type=MESH)

    def first_direct(m):
        row, along = SLOT_FROM[m]
        return pltpu.make_async_remote_copy(
            src_ref=xg.at[block(0), slot(0)], dst_ref=xg.at[block(0), slot(m)],
            send_sem=first_send, recv_sem=hand_recv.at[0, 1] if m == 1 else ag_recv.at[0, m // 2 - 1],
            device_id=(0, grp, at(row, 4 - along)), device_id_type=MESH)

    def next_copy(b, m):
        return pltpu.make_async_remote_copy(
            src_ref=xo.at[block(b)], dst_ref=xg.at[block(b), slot(m)],
            send_sem=next_send, recv_sem=hand_recv.at[b, m],
            device_id=(phase + 1, grp, (me, opposite)[m]), device_id_type=MESH)

    def forward_copy(b, n):
        return pltpu.make_async_remote_copy(
            src_ref=xg.at[block(b), slot(0, 2)], dst_ref=xg.at[block(b), slot(2 * n + 2, 2)],
            send_sem=ag_send, recv_sem=ag_recv.at[b, n],
            device_id=(phase, grp, at(*NEIGHBOURS[n])), device_id_type=MESH)

    def part_copy(b, m):
        return pltpu.make_async_remote_copy(
            src_ref=st.at[m, block(b)], dst_ref=rs.at[m, block(b)],
            send_sem=rs_send, recv_sem=rs_recv.at[b],
            device_id=(phase, grp, target(m)), device_id_type=MESH)

    def waiter(buffer, send_sem, recv_sem):
        return pltpu.make_async_remote_copy(
            src_ref=buffer, dst_ref=buffer, send_sem=send_sem, recv_sem=recv_sem,
            device_id=(phase, grp, target(0)), device_id_type=MESH)

    def forward(b):
        pl.when(phase > 0)(waiter(xg.at[block(b), slot(0)], rs_send, hand_recv.at[b, 0]).wait_recv)
        waiter(xg.at[block(b), slot(1)], rs_send, hand_recv.at[b, 1]).wait_recv()

        @pl.when((phase > 0) | (b > 0))
        def _():
            for n in range(len(NEIGHBOURS)):
                forward_copy(b, n).start()

    middle = ((phase > 0) & (phase < N_PHASE - 1)).astype(jnp.int32)
    pl.semaphore_wait(barrier, SLOTS + N_GRP - 1 + 2 + 2 * middle)
    @pl.when(phase == 0)
    def _():
        own_rows.wait()
        for m in (5, 3, 7, 1, 4, 2, 6):
            first_direct(m).start()

    for copy in small:
        copy.wait()

    @pl.when(phase == 0)
    def _():
        xg[PTOK:ROWS, 0:CH] = jnp.concatenate(
            [steps_ref[j].astype(jnp.float32) for j in range(STEPS)], axis=0).astype(jnp.bfloat16)

        @pl.loop(1, NB)
        def _(b):
            first_copy(b).start()

    lens = [lens_ref[grp, d] for d in range(DOCS)]
    starts = [jnp.int32(0)]
    for d in range(DOCS):
        starts.append(starts[-1] + lens[d])

    def pick(values, index):
        out = jnp.full(index.shape, values[-1], jnp.int32)
        for d in range(DOCS - 1):
            out = jnp.where(index == d, values[d], out)
        return out

    def segment_and_place(row):
        of_prompt = sum((row >= starts[d]).astype(jnp.int32) for d in range(1, DOCS))
        of_step = (row - PTOK) & (DOCS - 1)
        step = (row - PTOK) >> 2
        segment = jnp.where(row < PTOK, of_prompt, of_step)
        place = jnp.where(row < PTOK, row - pick(starts[:DOCS], of_prompt), pick(lens, of_step) + step)
        return jnp.where(row < ROWS, segment, -1), place

    seg_q, place_q = segment_and_place(lax.broadcasted_iota(jnp.int32, (ROWS, HD), 0))
    lane = lax.broadcasted_iota(jnp.int32, (ROWS, HD), 1)
    half = (lane & (HD // 2 - 1)).astype(jnp.float32)
    angle = place_q.astype(jnp.float32) * jnp.exp(half * (-2.0 / HD * math.log(THETA)))
    cosb[...] = jnp.cos(angle)
    sine = jnp.sin(angle)
    sinb[...] = jnp.where(lane < HD // 2, -sine, sine)
    for part in range(KEYS // HD):
        seg_k, place_k = segment_and_place(lax.broadcasted_iota(jnp.int32, (ROWS, HD), 1) + part * HD)
        bias[:, part * HD : (part + 1) * HD] = jnp.where((seg_q == seg_k) & (place_k <= place_q), 0.0, -1e30)
    row = lax.broadcasted_iota(jnp.int32, (N_GRP * STEPS * CAP, STEPS * DOCS), 0)
    col = lax.broadcasted_iota(jnp.int32, (N_GRP * STEPS * CAP, STEPS * DOCS), 1)
    dests = [dest_ref[grp, d] for d in range(DOCS)]
    ranks = [
        sum([(dests[e] == dests[d]).astype(jnp.int32) for e in range(d)], jnp.int32(0)) for d in range(DOCS)
    ]
    doc = col & (DOCS - 1)
    chosen = (
        (pick(dests, doc) == (row >> 3)) & (pick(ranks, doc) == (row & 1)) & ((col >> 2) == ((row >> 1) & 3))
    )
    choice[...] = jnp.where(chosen, 1.0, 0.0).astype(jnp.bfloat16)
    kb[...] = jnp.zeros_like(kb)
    vb[:, 0:HD] = jnp.zeros((KEYS, HD), jnp.bfloat16)
    vb[:, HD:] = jnp.ones((KEYS, HD), jnp.bfloat16)
    for m in range(N_TP):
        for copy in weight_copies(m):
            copy.wait()

    def project_in(b):
        def pass_on():
            @pl.when(b < NB - ahead)
            def _():
                forward(b + ahead)

        total, squared = None, None
        for m in range(N_TP):
            if m == PASS_ON_AT:
                pass_on()
            if m > 1 and m % 2 == 0:
                waiter(xg.at[block(b), slot(m, 2)], rs_send, ag_recv.at[b, m // 2 - 1]).wait_recv()
            values = xg[block(b), m * CH : (m + 1) * CH].astype(jnp.float32)
            squares = values * values
            piece = sum(squares[:, i * HD : (i + 1) * HD] for i in range(CH // HD))
            scaled = (values * gain_ref[:, m * CH : (m + 1) * CH]).astype(jnp.bfloat16)
            product = jnp.dot(scaled, w[m * CH : (m + 1) * CH, :], preferred_element_type=jnp.float32)
            total = product if total is None else total + product
            squared = piece if squared is None else squared + piece
        return total * lax.rsqrt(jnp.sum(squared, axis=-1, keepdims=True) * (1.0 / D) + EPS)

    def attend(b, projected):
        cosine, sine = cosb[block(b)], sinb[block(b)]

        def rotated(values):
            return (values * cosine + pltpu.roll(values, HD // 2, 1) * sine).astype(jnp.bfloat16)

        heads = [rotated(projected[:, h * HD : (h + 1) * HD]) for h in range(HQ + 1)]
        kb[block(b)] = heads[HQ]
        vb[block(b), 0:HD] = projected[:, (HQ + 1) * HD :].astype(jnp.bfloat16)
        queries = jnp.concatenate(heads[:HQ], axis=0)
        scores = lax.dot_general(
            queries, kb[...], (((1,), (1,)), ((), ())), preferred_element_type=jnp.float32)
        scores = scores * (1.0 / math.sqrt(HD)) + jnp.concatenate([bias[block(b)]] * HQ, axis=0)
        raised = jnp.exp(scores - jnp.max(scores, axis=-1, keepdims=True)).astype(jnp.bfloat16)
        mixed = jnp.dot(raised, vb[...], preferred_element_type=jnp.float32)
        mixed = (mixed[:, 0:HD] / mixed[:, HD:]).astype(jnp.bfloat16)
        return jnp.concatenate([mixed[h * R : (h + 1) * R] for h in range(HQ)], axis=1)

    def finish(b):
        waiter(rs.at[:, block(b)], rs_send, rs_recv.at[b]).wait_recv()
        total = own[b % 2]
        for m in range(SLOTS):
            total += rs[m, block(b)].astype(jnp.float32)
        xo[block(b)] = total.astype(jnp.bfloat16)

        @pl.when(phase < N_PHASE - 1)
        def _():
            next_copy(b, 1).start()
            next_copy(b, 0).start()

    def project_out(b, heads):
        def product(m):
            return jnp.dot(heads, wo[:, m * CH : (m + 1) * CH], preferred_element_type=jnp.float32)

        ready = product(0)
        for m in range(SLOTS):
            following = product(m + 1)
            st[m, block(b)] = ready.astype(jnp.bfloat16)
            part_copy(b, m).start()
            ready = following
        own[b % 2] = ready + xg[block(b), 0:CH].astype(jnp.float32)

    forward(0)

    @pl.when(phase == 0)
    def _():
        forward(1)

    @pl.loop(0, NB)
    def _(b):

        projected = project_in(b)
        heads = attend(b, projected)

        @pl.when(b == 0)
        def _():
            for m in range(N_TP):
                out_weight_copy(m).wait()

        project_out(b, heads)
        pl.when(b > 0)(functools.partial(finish, b - 1))


    finish(NB - 1)

    picked = jnp.dot(choice[...], xo[PTOK:ROWS], preferred_element_type=jnp.float32)
    for g in range(N_GRP):
        rows = picked[g * STEPS * CAP : (g + 1) * STEPS * CAP]
        dsend[g] = jnp.concatenate([rows[:, : CH // 2], rows[:, CH // 2 :]], axis=0).astype(jnp.bfloat16)

    def decode_copy(k):
        to = (grp + k) % N_GRP
        return pltpu.make_async_remote_copy(
            src_ref=dsend.at[to], dst_ref=drecv.at[grp],
            send_sem=dec_send.at[k], recv_sem=dec_recv.at[k],
            device_id=(phase, to, me), device_id_type=MESH)

    for k in range(1, N_GRP):
        decode_copy(k).start()
    n = N_GRP * STEPS * CAP
    row = lax.broadcasted_iota(jnp.int32, (n, 2 * n), 0)
    col = lax.broadcasted_iota(jnp.int32, (n, 2 * n), 1)
    wanted = ((row >> 1) & 3) * 16 + (row >> 3) * 2 + (row & 1)
    orders = [jnp.where(col == wanted + part * STEPS * CAP, 1.0, 0.0).astype(jnp.bfloat16) for part in range(2)]
    drecv[grp] = dsend[grp]
    pre_out[...] = xo[0:PTOK]

    @pl.when(phase == 0)
    def _():
        waiter(xg.at[:, slot(0)], first_send, rs_recv.at[0]).wait_send()
        waiter(xg.at[block(0), slot(0, 6)], first_send, rs_recv.at[0]).wait_send()
        waiter(xg.at[pl.ds(R, ROWS - R), slot(0, 6)], ag_send, rs_recv.at[0]).wait_send()

    @pl.when(phase < N_PHASE - 1)
    def _():
        waiter(xg.at[:, slot(0, 2)], next_send, rs_recv.at[0]).wait_send()

    @pl.when(phase > 0)
    def _():
        waiter(xg.at[:, slot(0, 6)], ag_send, rs_recv.at[0]).wait_send()

    waiter(st, rs_send, rs_recv.at[0]).wait_send()

    for k in range(1, N_GRP):
        came = (grp + N_GRP - k) % N_GRP
        pltpu.make_async_remote_copy(
            src_ref=dsend.at[came], dst_ref=drecv.at[came],
            send_sem=dec_send.at[k], recv_sem=dec_recv.at[k],
            device_id=(phase, came, me), device_id_type=MESH).wait_recv()
        decode_copy(k).wait_send()
    received = drecv[...].reshape(2 * n, CH // 2)
    for part in range(2):
        arranged = jnp.dot(orders[part], received, preferred_element_type=jnp.float32)
        dec_out[:, :, part * (CH // 2) : (part + 1) * (CH // 2)] = arranged.reshape(
            STEPS, N_GRP * CAP, CH // 2).astype(jnp.bfloat16)


def body(
    prompt_embed, prompt_lengths, decode_group, step_embed, norm_gain, w_query, w_key, w_value, w_out,
):
    vmem = pl.BlockSpec(memory_space=pltpu.VMEM)
    hbm = pl.BlockSpec(memory_space=pl.ANY)
    bf16, f32 = jnp.bfloat16, jnp.float32
    dma = pltpu.SemaphoreType.DMA
    prefill, decode = pl.pallas_call(
        kernel,
        name="layers",
        out_shape=(
            jax.ShapeDtypeStruct((PTOK, CH), bf16),
            jax.ShapeDtypeStruct((STEPS, N_GRP * CAP, CH), bf16),
        ),
        in_specs=[hbm] * 9,
        out_specs=(vmem, vmem),
        scratch_shapes=[
            pltpu.SMEM((N_GRP, DOCS), jnp.int32),
            pltpu.SMEM((N_GRP, DOCS), jnp.int32),
            pltpu.VMEM((STEPS, DOCS, CH), bf16),
            pltpu.VMEM((1, D), f32),
            pltpu.VMEM((D, NQKV), bf16),
            pltpu.VMEM((HQ * HD, D), bf16),
            pltpu.VMEM((ROWS, D), bf16),
            pltpu.VMEM((SLOTS, ROWS, CH), bf16),
            pltpu.VMEM((SLOTS, ROWS, CH), bf16),
            pltpu.VMEM((ROWS, CH), bf16),
            pltpu.VMEM((2, R, CH), f32),
            pltpu.VMEM((N_GRP * STEPS * CAP, STEPS * DOCS), bf16),
            pltpu.VMEM((KEYS, HD), bf16),
            pltpu.VMEM((KEYS, 2 * HD), bf16),
            pltpu.VMEM((ROWS, HD), f32),
            pltpu.VMEM((ROWS, HD), f32),
            pltpu.VMEM((ROWS, KEYS), f32),
            pltpu.VMEM((N_GRP, 2 * STEPS * CAP, CH // 2), bf16),
            pltpu.VMEM((N_GRP, 2 * STEPS * CAP, CH // 2), bf16),
            dma((4,)),
            dma((5, N_TP)),
            dma(()),
            dma(()),
            dma((NB, 2)),
            dma(()),
            dma((NB, len(NEIGHBOURS))),
            dma(()),
            dma((NB,)),
            dma((N_GRP,)),
            dma((N_GRP,)),
        ],
        compiler_params=pltpu.CompilerParams(
            collective_id=0, has_side_effects=True, vmem_limit_bytes=60 << 20),
    )(
        prompt_lengths,
        decode_group.reshape(N_GRP, DOCS),
        prompt_embed,
        step_embed,
        norm_gain,
        w_query[0],
        w_key[0],
        w_value[0],
        w_out[0],
    )
    return prefill[None], decode[None]


def solution(mesh):
    return jax.shard_map(
        body,
        mesh=mesh,
        in_specs=(
            P("grp", "tp"),
            P(),
            P(),
            P(None, "grp", "tp"),
            P("phase", None),
            P("phase", None, "tp"),
            P("phase", None, "tp"),
            P("phase", None, "tp"),
            P("phase", "tp", None),
        ),
        out_specs=(P("phase", "grp", "tp"), P("phase", None, "grp", "tp")),
        check_vma=False,
    )
```
